512 devices in a mesh: row: 32 (over y, x, core), col: 16 (over z).
Axes of the slice: x: 4, y: 4, z: 16, core: 2. Of those that a mesh axis runs over, the one named last changes fastest.
Arguments:
- ainv_block: float32 [4096, 4096], P('row', 'col'), as said below
- factor: float32 [2, 4096, 1024], P(None, 'row', 'col'), may hold values from -0.8 to 0.8
- block_mask: int32 [2, 32], replicated, may hold values 0 or 1
- diag_inverse: float32 [1024, 2, 1024], P('row', None, 'col'), may hold values from -6 to 6
Outputs:
- ainv_panel: float32 [1024, 2, 4096], P('col', None, 'row')
- ainv_diag: float32 [1024, 2, 1024], P('row', None, 'col')
The draws below stay inside these ranges and needn't reach their ends.
Inputs may be any that keep to these rules, and one draw needn't show every extreme that they name: `ainv_block`: symmetric, diagonal entries between 2 and 3, off-diagonal entries of order one over the square root of 4096.
All inputs are finite; a program needn't handle non-finite values.
Results may differ from the reference program's by a relative error of at most 0.0001.
Values sent between devices are 32-bit elements; how exact they have to be, the bound alone decides.
A program may use at most 64 MiB of HBM per device.

```python
import jax
import jax.numpy as jnp
from jax import lax

W = 1024
NODES = 2
BLOCK = 128
M = 4096
NBLK = 32


def draw_ainv_block(key, part):
    key_off = jax.random.fold_in(key, 11)
    key_diag = jax.random.fold_in(key, 12)
    raw = jax.random.normal(key_off, (M, M), jnp.float32)
    off = (raw + raw.T) * (0.7 / M ** 0.5)
    diag = 1.0 + 0.5 * jax.random.uniform(key_diag, (M,), jnp.float32)
    eye = jnp.eye(M, dtype=jnp.float32)
    return off * (1.0 - eye) + eye * diag[:, None] * 2.0


def touch_ends(entries, key, least, top_value):
    longest = entries.shape.index(max(entries.shape))
    spots = []
    for shift in (0, 1):
        where = [jax.random.randint(jax.random.fold_in(key, axis), (), 0, length) for axis, length in enumerate(entries.shape)]
        where[longest] = (where[longest] + shift) % entries.shape[longest]
        spots.append(tuple(where))
    return entries.at[spots[0]].set(least).at[spots[1]].set(top_value)


def block_scale(own_key, dims, split, low, largest):
    factor_of = 1.0
    for dim, parts in split:
        draws = jax.random.uniform(jax.random.fold_in(jax.random.fold_in(own_key, 6), dim), (parts,), jnp.float32, low / len(split), largest / len(split))
        factor_of = factor_of * jnp.repeat(jnp.exp(draws), dims[dim] // parts).reshape((-1,) + (1,) * (len(dims) - 1 - dim))
    return factor_of


def centred(stream_key, extent, width, bound, pieces=(), kind=jnp.bfloat16):
    entries = jax.random.normal(stream_key, extent, jnp.float32) * width
    if len(pieces) > 0:
        entries = block_scale(stream_key, extent, pieces, -0.22, 0.18) * entries
    return jnp.clip(entries, min=-bound, max=bound).astype(kind)


def setup_inputs(seed: int = 0) -> dict:
    streams_of = jax.random.split(jax.random.key(seed), 5)
    return {
        "ainv_block": draw_ainv_block(jax.random.fold_in(streams_of[4], 71), 0),
        "factor": centred(streams_of[1], (NODES, M, W), 0.1, 0.8, ((1, 32), (2, 16)), jnp.float32),
        "block_mask": touch_ends((jax.random.randint(streams_of[2], (NODES, NBLK), 0, 4) < 3).astype(jnp.int32), jax.random.fold_in(streams_of[2], 1), 0, 1),
        "diag_inverse": centred(streams_of[3], (W, NODES, W), 1.0, 6.0, ((0, 32), (2, 16)), jnp.float32),
    }


def reference(ainv_block, factor, block_mask, diag_inverse):
    row_mask = jnp.repeat(block_mask, BLOCK, axis=1).astype(jnp.float32)
    masked = factor * row_mask[:, :, None]
    panels = []
    diags = []
    for node in range(NODES):
        product = jnp.dot(ainv_block, masked[node], precision=lax.Precision.HIGHEST, preferred_element_type=jnp.float32)
        panel = -(product * row_mask[node][:, None])
        correction = jnp.dot(masked[node].T, panel, precision=lax.Precision.HIGHEST, preferred_element_type=jnp.float32)
        panels.append(panel.T)
        diags.append(diag_inverse[:, node, :] - correction)
    return jnp.stack(panels, axis=1), jnp.stack(diags, axis=1)
```

```python
import jax
import jax.numpy as jnp
from jax import lax
from jax.experimental import pallas as pl
from jax.experimental.pallas import tpu as pltpu
from jax.sharding import PartitionSpec as P

MESH = pl.DeviceIdType.MESH
SIDE = 4
CHIPS = SIDE * SIDE
DEPTH = 16
LANES = 128
HANDS = {0: (2, 1), 2: (4, 3), 4: (6, 5), 6: (8, 7)}
ORDER = (2, 1, 4, 3, 6, 5, 8, 7)


def split(x):
    high = x.astype(jnp.bfloat16)
    return high, (x - high.astype(jnp.float32)).astype(jnp.bfloat16)


def signs(d):
    return (d,) if d in (0, 8) else (d, -d)


def slot(d):
    return (d + 7) % DEPTH


def kernel(
    a_ref, f_ref, mask_ref, diag_ref, panel_ref, out_ref,
    g, lhs_hi, lhs_lo, a_hi, a_lo, own, give, take, red, got, fin, pin, p_hi, p_lo,
    part, c_take, c_red, c_got,
    z_send, z_recv, x_send, x_recv, r_send, r_recv, t_send, t_recv, c_sems,
):
    row, col = lax.axis_index("row"), lax.axis_index("col")
    core = lax.rem(row, 2)
    chip = row // 2
    cy, cx = chip // SIDE, lax.rem(chip, SIDE)
    mate = (row + 1 - 2 * core, col)

    def along(d):
        return (row, lax.rem(col + d + DEPTH, DEPTH))

    def in_plane(i):
        return lax.rem(cy + i // SIDE, SIDE) * SIDE + lax.rem(cx + i % SIDE, SIDE)

    barrier = pltpu.get_barrier_semaphore()
    for who in [along(d) for d in (1, -1, 2, -2)] + [mate] + [(in_plane(i) * 2 + core, col) for i in range(1, CHIPS)]:
        pl.semaphore_signal(barrier, inc=1, device_id=who, device_id_type=MESH)

    keep = [mask_ref[s, row].astype(jnp.float32) for s in (0, 1)]
    for s in (0, 1):
        g[slot(0), 64 * s : 64 * s + 64] = f_ref[64 * s : 64 * s + 64] * keep[s]
    for half in (0, 1):
        which = pl.multiple_of(lax.rem(core + half, 2) * LANES, LANES)
        hi, lo = split(a_ref[:, pl.ds(which, LANES)])
        a_hi[:, half * LANES : half * LANES + LANES] = hi
        a_lo[:, half * LANES : half * LANES + LANES] = lo
    p_hi[...] = jnp.zeros_like(p_hi)
    p_lo[...] = jnp.zeros_like(p_lo)
    pl.semaphore_wait(barrier, 4 + 1 + CHIPS - 1)

    def hop(a, b):
        return pltpu.make_async_remote_copy(
            g.at[slot(a)], g.at[slot(b)], z_send.at[slot(b)], z_recv.at[slot(b)],
            device_id=along(b - a), device_id_type=MESH,
        )

    hops = {}

    def hand_on(a):
        step = 1 if a >= 0 else -1
        for b in HANDS.get(abs(a), ()):
            hops[b * step] = hop(a, b * step)
            hops[b * step].start()
            if a == 0:
                hops[-b] = hop(0, -b)
                hops[-b].start()

    def arrive(t):
        for d in signs(t):
            hops[d].wait_recv()
            if not (d == -6):
                hand_on(d)
            else:
                hops[-7] = hop(-6, -7)
                hops[-7].start()

    def swap(t):
        n = len(signs(t))
        return pltpu.make_async_remote_copy(
            give.at[t, pl.ds(0, n)], take.at[t, pl.ds(0, n)], x_send.at[t], x_recv.at[t],
            device_id=mate, device_id_type=MESH,
        )

    def multiply(t):
        for n, d in enumerate(signs(t)):
            hi, lo = split(g[slot(d)])
            for s in (0, 1):
                lhs_hi[slot(d), :, s * LANES : s * LANES + LANES] = hi[64 * s : 64 * s + 64]
                lhs_lo[slot(d), :, s * LANES : s * LANES + LANES] = lo[64 * s : 64 * s + 64]
            ah, al = a_hi[...], a_lo[...]
            x = jnp.dot(hi, ah, preferred_element_type=jnp.float32)
            x += jnp.dot(hi, al, preferred_element_type=jnp.float32)
            x += jnp.dot(lo, ah, preferred_element_type=jnp.float32)
            own[t, n] = x[:, :LANES]
            give[t, n] = x[:, LANES:]
        swap(t).start()

    def piece(t, i):
        n = len(signs(t))
        to = in_plane(i)
        return pltpu.make_async_remote_copy(
            red.at[t, to, pl.ds(0, n)], got.at[t, i, pl.ds(0, n)], r_send.at[t], r_recv.at[t],
            device_id=(to * 2 + core, col), device_id_type=MESH,
        )

    def scatter(t):
        swap(t).wait_recv()
        for n, _ in enumerate(signs(t)):
            red[t, :, n] = (own[t, n] + take[t, n]).reshape(CHIPS, 8, LANES)
        for i in range(1, CHIPS):
            piece(t, i).start()

    def home(t, n, d):
        return pltpu.make_async_remote_copy(
            fin.at[t, n], pin.at[chip], t_send, t_recv,
            device_id=(col * 2 + core, lax.rem(col - d + DEPTH, DEPTH)), device_id_type=MESH,
        )

    def finish(t):
        n = len(signs(t))
        arrived = got.at[t, pl.ds(1, CHIPS - 1), pl.ds(0, n)]
        pltpu.make_async_copy(arrived, arrived, r_recv.at[t]).wait()
        for n, d in enumerate(signs(t)):
            total = red[t, chip, n]
            for i in range(1, CHIPS):
                total += got[t, i, n]
            fin[t, n] = total
            if d != 0:
                home(t, n, d).start()
            else:
                @pl.when(chip != col)
                def _():
                    home(0, 0, 0).start()

                @pl.when(chip == col)
                def _():
                    pltpu.make_async_copy(fin.at[0, 0], pin.at[chip], t_recv).start()

    hand_on(0)
    stages = [(0, multiply), (2, arrive), (2, multiply), (0, scatter), (1, arrive), (1, multiply), (2, scatter)]
    stages += [(4, arrive), (4, multiply), (1, scatter), (0, finish), (3, arrive), (3, multiply), (4, scatter), (2, finish)]
    stages += [(6, arrive), (6, multiply), (3, scatter), (1, finish), (5, arrive), (5, multiply), (6, scatter), (4, finish)]
    stages += [(8, arrive), (8, multiply), (5, scatter), (3, finish), (7, arrive), (7, multiply), (8, scatter), (7, scatter)]
    stages += [(6, finish), (5, finish), (8, finish), (7, finish)]
    for t, what in stages:
        what(t)

    pltpu.make_async_copy(pin, pin, t_recv).wait()
    for s in (0, 1):
        block = pin[8 * s : 8 * s + 8].reshape(64, LANES) * keep[s]
        panel_ref[pl.ds(s, 64, stride=2), :] = -block
        hi, lo = split(block)
        p_hi[64 * s : 64 * s + 64, s * LANES : s * LANES + LANES] = hi
        p_lo[64 * s : 64 * s + 64, s * LANES : s * LANES + LANES] = lo

    contract = (((1,), (1,)), ((), ()))
    for n in range(4):
        span = slice(4 * n, 4 * n + 4)
        hi = lhs_hi[span].reshape(256, 2 * LANES)
        lo = lhs_lo[span].reshape(256, 2 * LANES)
        y = lax.dot_general(hi, p_hi[...], contract, preferred_element_type=jnp.float32)
        y += lax.dot_general(hi, p_lo[...], contract, preferred_element_type=jnp.float32)
        y += lax.dot_general(lo, p_hi[...], contract, preferred_element_type=jnp.float32)
        part[span] = y.reshape(4, 2, 32, LANES)

    c_swap = pltpu.make_async_remote_copy(
        part.at[:, 1 - core], c_take, c_sems.at[0], c_sems.at[1], device_id=mate, device_id_type=MESH
    )
    c_swap.start()
    c_swap.wait_recv()
    c_red[...] = part[:, core] + c_take[...]

    def c_piece(i):
        to = in_plane(i)
        return pltpu.make_async_remote_copy(
            c_red.at[lax.rem(col - to + 7 + 2 * DEPTH, DEPTH)], c_got.at[i], c_sems.at[2], c_sems.at[3],
            device_id=(to * 2 + core, col), device_id_type=MESH,
        )

    for i in range(1, CHIPS):
        c_piece(i).start()
    arrived = c_got.at[pl.ds(1, CHIPS - 1)]
    pltpu.make_async_copy(arrived, arrived, c_sems.at[3]).wait()
    total = c_red[lax.rem(col - chip + 7 + 2 * DEPTH, DEPTH)]
    for i in range(1, CHIPS):
        total += c_got[i]
    for s in (0, 1):
        rows = pl.ds(s, 32, stride=2)
        out_ref[rows, :] = diag_ref[rows, :] + total[:, 64 * s : 64 * s + 64]

    for d in hops:
        hops[d].wait_send()
    for t in range(9):
        swap(t).wait_send()
        n = len(signs(t))
        left = got.at[t, pl.ds(1, CHIPS - 1), pl.ds(0, n)]
        pltpu.make_async_copy(left, left, r_send.at[t]).wait()

    @pl.when(chip != col)
    def _():
        pltpu.make_async_copy(pin, pin, t_send).wait()

    @pl.when(chip == col)
    def _():
        left = pin.at[pl.ds(0, CHIPS - 1)]
        pltpu.make_async_copy(left, left, t_send).wait()

    c_swap.wait_send()
    pltpu.make_async_copy(arrived, arrived, c_sems.at[2]).wait()


def local(ainv_block, factor, block_mask, diag_inverse):
    f = jnp.transpose(factor, (0, 2, 1)).reshape(128, 128)
    diag = diag_inverse.reshape(64, 64)
    f32, bf16 = jnp.float32, jnp.bfloat16
    vmem = pl.BlockSpec(memory_space=pltpu.VMEM)
    dma = pltpu.SemaphoreType.DMA
    panel, out = pl.pallas_call(
        kernel,
        out_shape=(jax.ShapeDtypeStruct((128, 128), f32), jax.ShapeDtypeStruct((64, 64), f32)),
        in_specs=[vmem, vmem, pl.BlockSpec(memory_space=pltpu.SMEM), vmem],
        out_specs=(vmem, vmem),
        scratch_shapes=[
            pltpu.VMEM((DEPTH, 128, LANES), f32),
            pltpu.VMEM((DEPTH, 64, 256), bf16),
            pltpu.VMEM((DEPTH, 64, 256), bf16),
            pltpu.VMEM((128, 256), bf16),
            pltpu.VMEM((128, 256), bf16),
            pltpu.VMEM((9, 2, 128, LANES), f32),
            pltpu.VMEM((9, 2, 128, LANES), f32),
            pltpu.VMEM((9, 2, 128, LANES), f32),
            pltpu.VMEM((9, CHIPS, 2, 8, LANES), f32),
            pltpu.VMEM((9, CHIPS, 2, 8, LANES), f32),
            pltpu.VMEM((9, 2, 8, LANES), f32),
            pltpu.VMEM((CHIPS, 8, LANES), f32),
            pltpu.VMEM((128, 256), bf16),
            pltpu.VMEM((128, 256), bf16),
            pltpu.VMEM((DEPTH, 2, 32, LANES), f32),
            pltpu.VMEM((DEPTH, 32, LANES), f32),
            pltpu.VMEM((DEPTH, 32, LANES), f32),
            pltpu.VMEM((CHIPS, 32, LANES), f32),
            dma((DEPTH,)), dma((DEPTH,)), dma((9,)), dma((9,)), dma((9,)), dma((9,)), dma, dma, dma((4,)),
        ],
        compiler_params=pltpu.CompilerParams(collective_id=0, has_side_effects=True, vmem_limit_bytes=40 * 2**20),
        cost_estimate=pl.CostEstimate(flops=3 * 2 * 84 * 2**20, bytes_accessed=2**20, transcendentals=0),
    )(ainv_block, f, block_mask, diag)
    return panel.reshape(64, 2, 128), out.reshape(32, 2, 64)


def solution(mesh):
    placed = (P("row", "col"), P(None, "row", "col"), P(), P("row", None, "col"))
    return jax.shard_map(
        local,
        mesh=mesh,
        in_specs=placed,
        out_specs=(P("col", None, "row"), P("row", None, "col")),
        check_vma=False,
    )
```

```python
import jax
import jax.numpy as jnp
from jax import lax
from jax.experimental import pallas as pl
from jax.experimental.pallas import tpu as pltpu
from jax.sharding import PartitionSpec as P

MESH = pl.DeviceIdType.MESH
SIDE = 4
CHIPS = SIDE * SIDE
DEPTH = 16
LANES = 128
PARTS = 4
HANDS = {0: (2, 1), 2: (4, 3), 4: (6, 5), 6: (8, 7)}
ORDER = (2, 1, 4, 3, 6, 5, 8, 7)


def far(i):
    return min(i // SIDE, SIDE - i // SIDE) + min(i % SIDE, SIDE - i % SIDE)


OTHERS = sorted(range(1, CHIPS), key=far, reverse=True)


def split(x):
    high = x.astype(jnp.bfloat16)
    return high, (x - high.astype(jnp.float32)).astype(jnp.bfloat16)


def signs(d):
    return (d,) if d in (0, 8) else (d, -d)


def slot(d):
    return (d + 7) % DEPTH


def kernel(
    a_hbm, f_hbm, mask_hbm, diag_hbm, panel_ref, out_ref,
    a_ref, f_ref, mask_ref, diag_ref,
    g, lhs_hi, lhs_lo, a_hi, a_lo, own, give, take, red, got, fin, pin, p_hi, p_lo,
    part, c_take, c_red, c_got,
    in_sems, z_send, z_recv, x_send, x_recv, r_send, r_recv, t_send, t_recv, cx_send, cx_recv, c_sems,
):
    row, col = lax.axis_index("row"), lax.axis_index("col")
    core = lax.rem(row, 2)
    chip = row // 2
    cy, cx = chip // SIDE, lax.rem(chip, SIDE)
    mate = (row + 1 - 2 * core, col)

    def along(d):
        return (row, lax.rem(col + d + DEPTH, DEPTH))

    def in_plane(i):
        return lax.rem(cy + i // SIDE, SIDE) * SIDE + lax.rem(cx + i % SIDE, SIDE)

    loads = [
        pltpu.make_async_copy(mask_hbm, mask_ref, in_sems.at[0]),
        pltpu.make_async_copy(f_hbm, f_ref, in_sems.at[1]),
        pltpu.make_async_copy(a_hbm, a_ref, in_sems.at[2]),
        pltpu.make_async_copy(diag_hbm, diag_ref, in_sems.at[3]),
    ]
    for load in loads:
        load.start()
    barrier = pltpu.get_barrier_semaphore()
    for who in [along(d) for d in (1, -1, 2, -2)] + [mate] + [(in_plane(i) * 2 + core, col) for i in range(1, CHIPS)]:
        pl.semaphore_signal(barrier, inc=1, device_id=who, device_id_type=MESH)

    for load in loads:
        load.wait()
    keep = [mask_ref[s, row].astype(jnp.float32) for s in (0, 1)]
    for s in (0, 1):
        g[slot(0), 64 * s : 64 * s + 64] = f_ref[64 * s : 64 * s + 64] * keep[s]
    for half in (0, 1):
        which = pl.multiple_of(lax.rem(core + half, 2) * LANES, LANES)
        hi, lo = split(a_ref[:, pl.ds(which, LANES)])
        a_hi[:, half * LANES : half * LANES + LANES] = hi
        a_lo[:, half * LANES : half * LANES + LANES] = lo
    p_hi[...] = jnp.zeros_like(p_hi)
    p_lo[...] = jnp.zeros_like(p_lo)
    pl.semaphore_wait(barrier, 4 + 1 + CHIPS - 1)

    def hop(a, b):
        source, dest = g.at[slot(a)], g.at[slot(b)]
        if abs(b) == 8:
            half = pl.ds(0 if b > 0 else 64, 64)
            source, dest = g.at[slot(a), half], g.at[slot(b), half]
        return pltpu.make_async_remote_copy(
            source, dest, z_send.at[b + 8], z_recv.at[b + 8], device_id=along(b - a), device_id_type=MESH
        )

    hops = {}

    def hand_on(a):
        step = 1 if a >= 0 else -1
        for b in HANDS.get(abs(a), ()):
            hops[b * step] = hop(a, b * step)
            hops[b * step].start()
            if a == 0:
                hops[-b] = hop(0, -b)
                hops[-b].start()

    def arrive(t):
        for d in (t, -t):
            hops[d].wait_recv()
            hand_on(d)

    def swap(t):
        n = len(signs(t))
        return pltpu.make_async_remote_copy(
            give.at[t, pl.ds(0, n)], take.at[t, pl.ds(0, n)], x_send.at[t], x_recv.at[t],
            device_id=mate, device_id_type=MESH,
        )

    def multiply(t):
        for n, d in enumerate(signs(t)):
            hi, lo = split(g[slot(d)])
            for s in (0, 1):
                lhs_hi[slot(d), :, s * LANES : s * LANES + LANES] = hi[64 * s : 64 * s + 64]
                lhs_lo[slot(d), :, s * LANES : s * LANES + LANES] = lo[64 * s : 64 * s + 64]
            ah, al = a_hi[...], a_lo[...]
            x = jnp.dot(hi, ah, preferred_element_type=jnp.float32)
            x += jnp.dot(hi, al, preferred_element_type=jnp.float32)
            x += jnp.dot(lo, ah, preferred_element_type=jnp.float32)
            own[t, n] = x[:, :LANES]
            give[t, n] = x[:, LANES:]
        swap(t).start()

    def piece(t, i):
        n = len(signs(t))
        to = in_plane(i)
        return pltpu.make_async_remote_copy(
            red.at[t, to, pl.ds(0, n)], got.at[t, i, pl.ds(0, n)], r_send.at[t], r_recv.at[t],
            device_id=(to * 2 + core, col), device_id_type=MESH,
        )

    def scatter(t):
        swap(t).wait_recv()
        for n, _ in enumerate(signs(t)):
            red[t, :, n] = (own[t, n] + take[t, n]).reshape(CHIPS, 8, LANES)
        for i in OTHERS:
            piece(t, i).start()

    def home(t, n, d):
        return pltpu.make_async_remote_copy(
            fin.at[t, n], pin.at[chip], t_send, t_recv,
            device_id=(col * 2 + core, lax.rem(col - d + DEPTH, DEPTH)), device_id_type=MESH,
        )

    def finish(t):
        n = len(signs(t))
        arrived = got.at[t, pl.ds(1, CHIPS - 1), pl.ds(0, n)]
        pltpu.make_async_copy(arrived, arrived, r_recv.at[t]).wait()
        for n, d in enumerate(signs(t)):
            total = red[t, chip, n]
            for i in range(1, CHIPS):
                total += got[t, i, n]
            fin[t, n] = total
            if d != 0:
                home(t, n, d).start()
            else:
                @pl.when(chip != col)
                def _():
                    home(0, 0, 0).start()

                @pl.when(chip == col)
                def _():
                    pltpu.make_async_copy(fin.at[0, 0], pin.at[chip], t_recv).start()

    hand_on(0)
    stages = [(0, multiply), (2, arrive), (2, multiply), (1, arrive), (1, multiply), (4, arrive), (0, scatter), (2, scatter), (1, scatter), (4, multiply), (3, arrive), (3, multiply), (6, arrive), (4, scatter), (3, scatter), (6, multiply), (5, arrive), (5, multiply), (0, finish), (2, finish), (1, finish), (6, scatter), (5, scatter), (8, arrive), (8, multiply), (7, arrive), (7, multiply), (8, scatter), (7, scatter), (4, finish), (3, finish), (6, finish), (5, finish), (8, finish), (7, finish)]
    for t, what in stages:
        what(t)

    pltpu.make_async_copy(pin, pin, t_recv).wait()
    for s in (0, 1):
        block = pin[8 * s : 8 * s + 8].reshape(64, LANES) * keep[s]
        panel_ref[pl.ds(s, 64, stride=2), :] = -block
        hi, lo = split(block)
        p_hi[64 * s : 64 * s + 64, s * LANES : s * LANES + LANES] = hi
        p_lo[64 * s : 64 * s + 64, s * LANES : s * LANES + LANES] = lo

    contract = (((1,), (1,)), ((), ()))
    many = DEPTH // PARTS

    def c_swap(n):
        span = pl.ds(many * n, many)
        return pltpu.make_async_remote_copy(
            part.at[span, 1 - core], c_take.at[span], cx_send.at[n], cx_recv.at[n], device_id=mate, device_id_type=MESH
        )

    def target(k):
        return lax.rem(col - k + 7 + 2 * DEPTH, DEPTH)

    def c_piece(k):
        return pltpu.make_async_remote_copy(
            c_red.at[k], c_got.at[chip], c_sems.at[0], c_sems.at[1],
            device_id=(target(k) * 2 + core, col), device_id_type=MESH,
        )

    for n in range(PARTS):
        span = slice(many * n, many * n + many)
        hi = lhs_hi[span].reshape(64 * many, 2 * LANES)
        lo = lhs_lo[span].reshape(64 * many, 2 * LANES)
        y = lax.dot_general(hi, p_hi[...], contract, preferred_element_type=jnp.float32)
        y += lax.dot_general(hi, p_lo[...], contract, preferred_element_type=jnp.float32)
        y += lax.dot_general(lo, p_hi[...], contract, preferred_element_type=jnp.float32)
        part[span] = y.reshape(many, 2, 32, LANES)
        c_swap(n).start()
    for n in range(PARTS):
        span = slice(many * n, many * n + many)
        c_swap(n).wait_recv()
        c_red[span] = part[span, core] + c_take[span]
        for k in range(many * n, many * n + many):
            @pl.when(target(k) != chip)
            def _():
                c_piece(k).start()
    most = c_got.at[pl.ds(0, CHIPS - 1)]
    pltpu.make_async_copy(most, most, c_sems.at[1]).wait()
    total = c_red[lax.rem(col - chip + 7 + 2 * DEPTH, DEPTH)]
    for i in range(CHIPS):
        total += jnp.where(chip == i, jnp.zeros_like(total), c_got[i])
    for s in (0, 1):
        rows = pl.ds(s, 32, stride=2)
        out_ref[rows, :] = diag_ref[rows, :] + total[:, 64 * s : 64 * s + 64]

    for d in hops:
        hops[d].wait_send()
    for t in range(9):
        swap(t).wait_send()
        n = len(signs(t))
        left = got.at[t, pl.ds(1, CHIPS - 1), pl.ds(0, n)]
        pltpu.make_async_copy(left, left, r_send.at[t]).wait()

    @pl.when(chip != col)
    def _():
        pltpu.make_async_copy(pin, pin, t_send).wait()

    @pl.when(chip == col)
    def _():
        left = pin.at[pl.ds(0, CHIPS - 1)]
        pltpu.make_async_copy(left, left, t_send).wait()

    for n in range(PARTS):
        c_swap(n).wait_send()
    pltpu.make_async_copy(most, most, c_sems.at[0]).wait()


def hand_out(panel_in, out_in, panel, out, sems):
    copies = [pltpu.make_async_copy(panel_in, panel, sems.at[0]), pltpu.make_async_copy(out_in, out, sems.at[1])]
    for copy in copies:
        copy.start()
    for copy in copies:
        copy.wait()


def local(ainv_block, factor, block_mask, diag_inverse):
    f = jnp.transpose(factor, (0, 2, 1)).reshape(128, 128)
    diag = diag_inverse.reshape(64, 64)
    f32, bf16 = jnp.float32, jnp.bfloat16
    vmem = pl.BlockSpec(memory_space=pltpu.VMEM)
    dma = pltpu.SemaphoreType.DMA
    panel, out = pl.pallas_call(
        kernel,
        out_shape=(jax.ShapeDtypeStruct((128, 128), f32), jax.ShapeDtypeStruct((64, 64), f32)),
        in_specs=[pl.BlockSpec(memory_space=pltpu.HBM)] * 4,
        out_specs=(vmem, vmem),
        scratch_shapes=[
            pltpu.VMEM((128, 256), f32),
            pltpu.VMEM((128, LANES), f32),
            pltpu.SMEM((2, 32), jnp.int32),
            pltpu.VMEM((64, 64), f32),
            pltpu.VMEM((DEPTH, 128, LANES), f32),
            pltpu.VMEM((DEPTH, 64, 256), bf16),
            pltpu.VMEM((DEPTH, 64, 256), bf16),
            pltpu.VMEM((128, 256), bf16),
            pltpu.VMEM((128, 256), bf16),
            pltpu.VMEM((9, 2, 128, LANES), f32),
            pltpu.VMEM((9, 2, 128, LANES), f32),
            pltpu.VMEM((9, 2, 128, LANES), f32),
            pltpu.VMEM((9, CHIPS, 2, 8, LANES), f32),
            pltpu.VMEM((9, CHIPS, 2, 8, LANES), f32),
            pltpu.VMEM((9, 2, 8, LANES), f32),
            pltpu.VMEM((CHIPS, 8, LANES), f32),
            pltpu.VMEM((128, 256), bf16),
            pltpu.VMEM((128, 256), bf16),
            pltpu.VMEM((DEPTH, 2, 32, LANES), f32),
            pltpu.VMEM((DEPTH, 32, LANES), f32),
            pltpu.VMEM((DEPTH, 32, LANES), f32),
            pltpu.VMEM((CHIPS, 32, LANES), f32),
            dma((4,)), dma((DEPTH + 1,)), dma((DEPTH + 1,)), dma((9,)), dma((9,)), dma((9,)), dma((9,)), dma, dma, dma((PARTS,)), dma((PARTS,)), dma((2,)),
        ],
        compiler_params=pltpu.CompilerParams(collective_id=0, has_side_effects=True, vmem_limit_bytes=63 * 2**20),
        cost_estimate=pl.CostEstimate(flops=3 * 2 * 84 * 2**20, bytes_accessed=2**20, transcendentals=0),
    )(ainv_block, f, block_mask, diag)
    hbm = pl.BlockSpec(memory_space=pltpu.HBM)
    panel, out = pl.pallas_call(
        hand_out,
        out_shape=(jax.ShapeDtypeStruct((128, 128), f32), jax.ShapeDtypeStruct((64, 64), f32)),
        in_specs=[vmem, vmem],
        out_specs=(hbm, hbm),
        scratch_shapes=[dma((2,))],
    )(panel, out)
    return panel.reshape(64, 2, 128), out.reshape(32, 2, 64)


def solution(mesh):
    placed = (P("row", "col"), P(None, "row", "col"), P(), P("row", None, "col"))
    return jax.shard_map(
        local,
        mesh=mesh,
        in_specs=placed,
        out_specs=(P("col", None, "row"), P("row", None, "col")),
        check_vma=False,
    )
```

```python
import jax
import jax.numpy as jnp
from jax import lax
from jax.experimental import pallas as pl
from jax.experimental.pallas import tpu as pltpu
from jax.sharding import PartitionSpec as P

MESH = pl.DeviceIdType.MESH
SIDE = 4
CHIPS = SIDE * SIDE
DEPTH = 16
LANES = 128
PARTS = 8
HANDS = {0: (2, 1), 2: (4, 3), 4: (6, 5), 6: (8, 7)}
ORDER = (2, 1, 4, 3, 6, 5, 8, 7)


def far(i):
    return min(i // SIDE, SIDE - i // SIDE) + min(i % SIDE, SIDE - i % SIDE)


OTHERS = sorted(range(1, CHIPS), key=far, reverse=True)


def split(x):
    high = x.astype(jnp.bfloat16)
    return high, (x - high.astype(jnp.float32)).astype(jnp.bfloat16)


def signs(d):
    return (d,) if d in (0, 8) else (d, -d)


def slot(d):
    return (d + 7) % DEPTH


def kernel(
    a_hbm, f_hbm, mask_hbm, diag_hbm, panel_ref, out_ref,
    a_ref, f_ref, mask_ref, diag_ref,
    g, lhs_hi, lhs_lo, a_hi, a_lo, own, give, take, red, got, fin, pin, p_hi, p_lo,
    part, c_take, c_red, c_got,
    in_sems, z_send, z_recv, x_send, x_recv, r_send, r_recv, t_send, t_recv, cx_send, cx_recv, c_sems, ready,
):
    row, col = lax.axis_index("row"), lax.axis_index("col")
    core = lax.rem(row, 2)
    chip = row // 2
    cy, cx = chip // SIDE, lax.rem(chip, SIDE)
    mate = (row + 1 - 2 * core, col)

    def along(d):
        return (row, lax.rem(col + d + DEPTH, DEPTH))

    def in_plane(i):
        return lax.rem(cy + i // SIDE, SIDE) * SIDE + lax.rem(cx + i % SIDE, SIDE)

    loads = [
        pltpu.make_async_copy(mask_hbm, mask_ref, in_sems.at[0]),
        pltpu.make_async_copy(f_hbm, f_ref, in_sems.at[1]),
        pltpu.make_async_copy(a_hbm, a_ref, in_sems.at[2]),
        pltpu.make_async_copy(diag_hbm, diag_ref, in_sems.at[3]),
    ]
    for load in loads:
        load.start()
    barrier = pltpu.get_barrier_semaphore()
    for who in [along(d) for d in (1, -1, 2, -2)] + [mate] + [(in_plane(i) * 2 + core, col) for i in (1, 2, 3, 4, 8, 12)]:
        pl.semaphore_signal(barrier, inc=1, device_id=who, device_id_type=MESH)

    for load in loads:
        load.wait()
    keep = [mask_ref[s, row].astype(jnp.float32) for s in (0, 1)]
    for s in (0, 1):
        g[slot(0), 64 * s : 64 * s + 64] = f_ref[64 * s : 64 * s + 64] * keep[s]
    for half in (0, 1):
        which = pl.multiple_of(lax.rem(core + half, 2) * LANES, LANES)
        hi, lo = split(a_ref[:, pl.ds(which, LANES)])
        a_hi[:, half * LANES : half * LANES + LANES] = hi
        a_lo[:, half * LANES : half * LANES + LANES] = lo
    p_hi[...] = jnp.zeros_like(p_hi)
    p_lo[...] = jnp.zeros_like(p_lo)
    pl.semaphore_wait(barrier, 4 + 1 + 6)

    def hop(a, b):
        source, dest = g.at[slot(a)], g.at[slot(b)]
        if abs(b) == 8:
            half = pl.ds(0 if b > 0 else 64, 64)
            source, dest = g.at[slot(a), half], g.at[slot(b), half]
        return pltpu.make_async_remote_copy(
            source, dest, z_send.at[b + 8], z_recv.at[b + 8], device_id=along(b - a), device_id_type=MESH
        )

    hops = {}

    def hand_on(a):
        step = 1 if a >= 0 else -1
        for b in HANDS.get(abs(a), ()):
            hops[b * step] = hop(a, b * step)
            hops[b * step].start()
            if a == 0:
                hops[-b] = hop(0, -b)
                hops[-b].start()

    def arrive(t):
        for d in (t, -t):
            hops[d].wait_recv()
            hand_on(d)

    def swap(t):
        n = len(signs(t))
        return pltpu.make_async_remote_copy(
            give.at[t, pl.ds(0, n)], take.at[t, pl.ds(0, n)], x_send.at[t], x_recv.at[t],
            device_id=mate, device_id_type=MESH,
        )

    def multiply(t):
        for n, d in enumerate(signs(t)):
            hi, lo = split(g[slot(d)])
            for s in (0, 1):
                lhs_hi[slot(d), :, s * LANES : s * LANES + LANES] = hi[64 * s : 64 * s + 64]
                lhs_lo[slot(d), :, s * LANES : s * LANES + LANES] = lo[64 * s : 64 * s + 64]
            ah, al = a_hi[...], a_lo[...]
            x = jnp.dot(hi, ah, preferred_element_type=jnp.float32)
            x += jnp.dot(hi, al, preferred_element_type=jnp.float32)
            x += jnp.dot(lo, ah, preferred_element_type=jnp.float32)
            own[t, n] = x[:, :LANES]
            give[t, n] = x[:, LANES:]
        swap(t).start()

    def piece(t, i):
        n = len(signs(t))
        to = in_plane(i)
        return pltpu.make_async_remote_copy(
            red.at[t, to, pl.ds(0, n)], got.at[t, i, pl.ds(0, n)], r_send.at[t], r_recv.at[t],
            device_id=(to * 2 + core, col), device_id_type=MESH,
        )

    def scatter(t):
        if t == 0:
            pl.semaphore_wait(ready, SIDE - 1)
        swap(t).wait_recv()
        for n, _ in enumerate(signs(t)):
            red[t, :, n] = (own[t, n] + take[t, n]).reshape(CHIPS, 8, LANES)
        for i in OTHERS:
            piece(t, i).start()

    def home(t, n, d):
        return pltpu.make_async_remote_copy(
            fin.at[t, n], pin.at[chip], t_send, t_recv,
            device_id=(col * 2 + core, lax.rem(col - d + DEPTH, DEPTH)), device_id_type=MESH,
        )

    def finish(t):
        n = len(signs(t))
        arrived = got.at[t, pl.ds(1, CHIPS - 1), pl.ds(0, n)]
        pltpu.make_async_copy(arrived, arrived, r_recv.at[t]).wait()
        for n, d in enumerate(signs(t)):
            total = red[t, chip, n]
            for i in range(1, CHIPS):
                total += got[t, i, n]
            fin[t, n] = total
            if d != 0:
                home(t, n, d).start()
            else:
                @pl.when(chip != col)
                def _():
                    home(0, 0, 0).start()

                @pl.when(chip == col)
                def _():
                    pltpu.make_async_copy(fin.at[0, 0], pin.at[chip], t_recv).start()

    hand_on(0)
    for i in (4, 8, 12):
        pl.semaphore_signal(ready, inc=1, device_id=(in_plane(i) * 2 + core, col), device_id_type=MESH)
    stages = [(0, multiply), (2, arrive), (2, multiply), (1, arrive), (0, scatter), (1, multiply), (2, scatter), (4, arrive), (4, multiply), (1, scatter), (3, arrive), (3, multiply), (4, scatter), (0, finish), (6, arrive), (6, multiply), (3, scatter), (2, finish), (5, arrive), (5, multiply), (6, scatter), (1, finish), (5, scatter), (4, finish), (8, arrive), (8, multiply), (7, arrive), (7, multiply), (8, scatter), (7, scatter), (3, finish), (6, finish), (5, finish), (8, finish), (7, finish)]
    for t, what in stages:
        what(t)

    pltpu.make_async_copy(pin, pin, t_recv).wait()
    for s in (0, 1):
        block = pin[8 * s : 8 * s + 8].reshape(64, LANES) * keep[s]
        panel_ref[pl.ds(s, 64, stride=2), :] = -block
        hi, lo = split(block)
        p_hi[64 * s : 64 * s + 64, s * LANES : s * LANES + LANES] = hi
        p_lo[64 * s : 64 * s + 64, s * LANES : s * LANES + LANES] = lo

    contract = (((1,), (1,)), ((), ()))
    many = CHIPS // PARTS
    order = OTHERS + [0]

    def c_swap(n):
        span = pl.ds(many * n, many)
        return pltpu.make_async_remote_copy(
            part.at[span, 1 - core], c_take.at[span], cx_send.at[n], cx_recv.at[n], device_id=mate, device_id_type=MESH
        )

    def block(half, i):
        to = in_plane(i) if i else chip
        return half[lax.rem(col - to + 7 + 2 * DEPTH, DEPTH)]

    def c_piece(k):
        i = order[k]
        return pltpu.make_async_remote_copy(
            c_red.at[k], c_got.at[k], c_sems.at[0], c_sems.at[1],
            device_id=(in_plane(i) * 2 + core, col), device_id_type=MESH,
        )

    for n in range(PARTS):
        span = slice(many * n, many * n + many)
        hi = jnp.concatenate([block(lhs_hi, i) for i in order[span]], axis=0)
        lo = jnp.concatenate([block(lhs_lo, i) for i in order[span]], axis=0)
        y = lax.dot_general(hi, p_hi[...], contract, preferred_element_type=jnp.float32)
        y += lax.dot_general(hi, p_lo[...], contract, preferred_element_type=jnp.float32)
        y += lax.dot_general(lo, p_hi[...], contract, preferred_element_type=jnp.float32)
        part[span] = y.reshape(many, 2, 32, LANES)
        c_swap(n).start()
    for n in range(PARTS):
        span = slice(many * n, many * n + many)
        c_swap(n).wait_recv()
        c_red[span] = part[span, core] + c_take[span]
        for k in range(many * n, many * n + many):
            if order[k]:
                c_piece(k).start()
    most = c_got.at[pl.ds(0, CHIPS - 1)]
    pltpu.make_async_copy(most, most, c_sems.at[1]).wait()
    total = c_red[CHIPS - 1]
    for k in range(CHIPS - 1):
        total += c_got[k]
    for s in (0, 1):
        rows = pl.ds(s, 32, stride=2)
        out_ref[rows, :] = diag_ref[rows, :] + total[:, 64 * s : 64 * s + 64]

    for d in hops:
        hops[d].wait_send()
    for t in range(9):
        swap(t).wait_send()
        n = len(signs(t))
        left = got.at[t, pl.ds(1, CHIPS - 1), pl.ds(0, n)]
        pltpu.make_async_copy(left, left, r_send.at[t]).wait()

    @pl.when(chip != col)
    def _():
        pltpu.make_async_copy(pin, pin, t_send).wait()

    @pl.when(chip == col)
    def _():
        left = pin.at[pl.ds(0, CHIPS - 1)]
        pltpu.make_async_copy(left, left, t_send).wait()

    for n in range(PARTS):
        c_swap(n).wait_send()
    pltpu.make_async_copy(most, most, c_sems.at[0]).wait()


def hand_out(panel_in, out_in, panel, out, sems):
    copies = [pltpu.make_async_copy(panel_in, panel, sems.at[0]), pltpu.make_async_copy(out_in, out, sems.at[1])]
    for copy in copies:
        copy.start()
    for copy in copies:
        copy.wait()


def local(ainv_block, factor, block_mask, diag_inverse):
    f = jnp.transpose(factor, (0, 2, 1)).reshape(128, 128)
    diag = diag_inverse.reshape(64, 64)
    f32, bf16 = jnp.float32, jnp.bfloat16
    vmem = pl.BlockSpec(memory_space=pltpu.VMEM)
    dma = pltpu.SemaphoreType.DMA
    panel, out = pl.pallas_call(
        kernel,
        out_shape=(jax.ShapeDtypeStruct((128, 128), f32), jax.ShapeDtypeStruct((64, 64), f32)),
        in_specs=[pl.BlockSpec(memory_space=pltpu.HBM)] * 4,
        out_specs=(vmem, vmem),
        scratch_shapes=[
            pltpu.VMEM((128, 256), f32),
            pltpu.VMEM((128, LANES), f32),
            pltpu.SMEM((2, 32), jnp.int32),
            pltpu.VMEM((64, 64), f32),
            pltpu.VMEM((DEPTH, 128, LANES), f32),
            pltpu.VMEM((DEPTH, 64, 256), bf16),
            pltpu.VMEM((DEPTH, 64, 256), bf16),
            pltpu.VMEM((128, 256), bf16),
            pltpu.VMEM((128, 256), bf16),
            pltpu.VMEM((9, 2, 128, LANES), f32),
            pltpu.VMEM((9, 2, 128, LANES), f32),
            pltpu.VMEM((9, 2, 128, LANES), f32),
            pltpu.VMEM((9, CHIPS, 2, 8, LANES), f32),
            pltpu.VMEM((9, CHIPS, 2, 8, LANES), f32),
            pltpu.VMEM((9, 2, 8, LANES), f32),
            pltpu.VMEM((CHIPS, 8, LANES), f32),
            pltpu.VMEM((128, 256), bf16),
            pltpu.VMEM((128, 256), bf16),
            pltpu.VMEM((DEPTH, 2, 32, LANES), f32),
            pltpu.VMEM((DEPTH, 32, LANES), f32),
            pltpu.VMEM((DEPTH, 32, LANES), f32),
            pltpu.VMEM((CHIPS, 32, LANES), f32),
            dma((4,)), dma((DEPTH + 1,)), dma((DEPTH + 1,)), dma((9,)), dma((9,)), dma((9,)), dma((9,)), dma, dma, dma((PARTS,)), dma((PARTS,)), dma((2,)), pltpu.SemaphoreType.REGULAR,
        ],
        compiler_params=pltpu.CompilerParams(collective_id=0, has_side_effects=True, vmem_limit_bytes=63 * 2**20),
        cost_estimate=pl.CostEstimate(flops=3 * 2 * 84 * 2**20, bytes_accessed=2**20, transcendentals=0),
    )(ainv_block, f, block_mask, diag)
    hbm = pl.BlockSpec(memory_space=pltpu.HBM)
    panel, out = pl.pallas_call(
        hand_out,
        out_shape=(jax.ShapeDtypeStruct((128, 128), f32), jax.ShapeDtypeStruct((64, 64), f32)),
        in_specs=[vmem, vmem],
        out_specs=(hbm, hbm),
        scratch_shapes=[dma((2,))],
    )(panel, out)
    return panel.reshape(64, 2, 128), out.reshape(32, 2, 64)


def solution(mesh):
    placed = (P("row", "col"), P(None, "row", "col"), P(), P("row", None, "col"))
    return jax.shard_map(
        local,
        mesh=mesh,
        in_specs=placed,
        out_specs=(P("col", None, "row"), P("row", None, "col")),
        check_vma=False,
    )
```

```python
import jax
import jax.numpy as jnp
from jax import lax
from jax.experimental import pallas as pl
from jax.experimental.pallas import tpu as pltpu
from jax.sharding import PartitionSpec as P

MESH = pl.DeviceIdType.MESH
SIDE = 4
CHIPS = SIDE * SIDE
DEPTH = 16
LANES = 128
PARTS = 8
HANDS = {0: (2, 1), 2: (4, 3), 4: (6, 5), 6: (8, 7)}
ORDER = (2, 1, 4, 3, 6, 5, 8, 7)


def far(i):
    return min(i // SIDE, SIDE - i // SIDE) + min(i % SIDE, SIDE - i % SIDE)


OTHERS = sorted(range(1, CHIPS), key=far, reverse=True)


def split(x):
    high = x.astype(jnp.bfloat16)
    return high, (x - high.astype(jnp.float32)).astype(jnp.bfloat16)


def signs(d):
    return (d,) if d in (0, 8) else (d, -d)


def slot(d):
    return (d + 7) % DEPTH


def kernel(
    a_hbm, f_hbm, mask_hbm, diag_hbm, panel_ref, out_ref,
    a_ref, f_ref, mask_ref, diag_ref,
    g, lhs_hi, lhs_lo, a_hi, a_lo, own, give, take, red, got, fin, pin, p_hi, p_lo,
    part, c_take, c_red, c_got,
    in_sems, z_send, z_recv, x_send, x_recv, r_send, r_recv, t_send, t_recv, cx_send, cx_recv, c_sems, ready,
):
    row, col = lax.axis_index("row"), lax.axis_index("col")
    core = lax.rem(row, 2)
    chip = row // 2
    cy, cx = chip // SIDE, lax.rem(chip, SIDE)
    mate = (row + 1 - 2 * core, col)

    def along(d):
        return (row, lax.rem(col + d + DEPTH, DEPTH))

    def in_plane(i):
        return lax.rem(cy + i // SIDE, SIDE) * SIDE + lax.rem(cx + i % SIDE, SIDE)

    loads = [
        pltpu.make_async_copy(mask_hbm, mask_ref, in_sems.at[0]),
        pltpu.make_async_copy(f_hbm, f_ref, in_sems.at[1]),
        pltpu.make_async_copy(a_hbm, a_ref, in_sems.at[2]),
        pltpu.make_async_copy(diag_hbm, diag_ref, in_sems.at[3]),
    ]
    for load in loads:
        load.start()
    barrier = pltpu.get_barrier_semaphore()
    for who in [along(d) for d in (1, -1, 2, -2)] + [mate] + [(in_plane(i) * 2 + core, col) for i in (1, 2, 3, 4, 8, 12)]:
        pl.semaphore_signal(barrier, inc=1, device_id=who, device_id_type=MESH)

    for load in loads:
        load.wait()
    keep = [mask_ref[s, row].astype(jnp.float32) for s in (0, 1)]
    for s in (0, 1):
        g[slot(0), 64 * s : 64 * s + 64] = f_ref[64 * s : 64 * s + 64] * keep[s]
    for half in (0, 1):
        which = pl.multiple_of(lax.rem(core + half, 2) * LANES, LANES)
        hi, lo = split(a_ref[:, pl.ds(which, LANES)])
        a_hi[:, half * LANES : half * LANES + LANES] = hi
        a_lo[:, half * LANES : half * LANES + LANES] = lo
    p_hi[...] = jnp.zeros_like(p_hi)
    p_lo[...] = jnp.zeros_like(p_lo)
    pl.semaphore_wait(barrier, 4 + 1 + 6)

    def hop(a, b):
        source, dest = g.at[slot(a)], g.at[slot(b)]
        if abs(b) == 8:
            half = pl.ds(0 if b > 0 else 64, 64)
            source, dest = g.at[slot(a), half], g.at[slot(b), half]
        return pltpu.make_async_remote_copy(
            source, dest, z_send.at[b + 8], z_recv.at[b + 8], device_id=along(b - a), device_id_type=MESH
        )

    hops = {}

    def hand_on(a):
        step = 1 if a >= 0 else -1
        for b in HANDS.get(abs(a), ()):
            hops[b * step] = hop(a, b * step)
            hops[b * step].start()
            if a == 0:
                hops[-b] = hop(0, -b)
                hops[-b].start()

    def arrive(t):
        for d in (t, -t):
            hops[d].wait_recv()
            hand_on(d)

    def swap(t):
        n = len(signs(t))
        return pltpu.make_async_remote_copy(
            give.at[t, pl.ds(0, n)], take.at[t, pl.ds(0, n)], x_send.at[t], x_recv.at[t],
            device_id=mate, device_id_type=MESH,
        )

    def multiply(t):
        for n, d in enumerate(signs(t)):
            hi, lo = split(g[slot(d)])
            for s in (0, 1):
                lhs_hi[slot(d), :, s * LANES : s * LANES + LANES] = hi[64 * s : 64 * s + 64]
                lhs_lo[slot(d), :, s * LANES : s * LANES + LANES] = lo[64 * s : 64 * s + 64]
            ah, al = a_hi[...], a_lo[...]
            x = jnp.dot(hi, ah, preferred_element_type=jnp.float32)
            x += jnp.dot(hi, al, preferred_element_type=jnp.float32)
            x += jnp.dot(lo, ah, preferred_element_type=jnp.float32)
            own[t, n] = x[:, :LANES]
            give[t, n] = x[:, LANES:]
        swap(t).start()

    def piece(t, i):
        n = len(signs(t))
        to = in_plane(i)
        return pltpu.make_async_remote_copy(
            red.at[t, to, pl.ds(0, n)], got.at[t, i, pl.ds(0, n)], r_send.at[t], r_recv.at[t],
            device_id=(to * 2 + core, col), device_id_type=MESH,
        )

    def scatter(t):
        if t == 0:
            pl.semaphore_wait(ready, SIDE - 1)
        swap(t).wait_recv()
        for n, _ in enumerate(signs(t)):
            red[t, :, n] = (own[t, n] + take[t, n]).reshape(CHIPS, 8, LANES)
        for i in OTHERS:
            piece(t, i).start()

    def home(t, n, d):
        return pltpu.make_async_remote_copy(
            fin.at[t, n], pin.at[chip], t_send, t_recv,
            device_id=(col * 2 + core, lax.rem(col - d + DEPTH, DEPTH)), device_id_type=MESH,
        )

    def finish(t):
        n = len(signs(t))
        arrived = got.at[t, pl.ds(1, CHIPS - 1), pl.ds(0, n)]
        pltpu.make_async_copy(arrived, arrived, r_recv.at[t]).wait()
        for n, d in enumerate(signs(t)):
            total = red[t, chip, n]
            for i in range(1, CHIPS):
                total += got[t, i, n]
            fin[t, n] = total
            if d != 0:
                home(t, n, d).start()
            else:
                @pl.when(chip != col)
                def _():
                    home(0, 0, 0).start()

                @pl.when(chip == col)
                def _():
                    pltpu.make_async_copy(fin.at[0, 0], pin.at[chip], t_recv).start()

    hand_on(0)
    for i in (4, 8, 12):
        pl.semaphore_signal(ready, inc=1, device_id=(in_plane(i) * 2 + core, col), device_id_type=MESH)
    stages = [(0, multiply), (2, arrive), (2, multiply), (1, arrive), (1, multiply), (0, scatter), (2, scatter), (4, arrive), (4, multiply), (1, scatter), (3, arrive), (3, multiply), (4, scatter), (0, finish), (6, arrive), (6, multiply), (3, scatter), (2, finish), (5, arrive), (5, multiply), (6, scatter), (1, finish), (5, scatter), (4, finish), (8, arrive), (8, multiply), (7, arrive), (7, multiply), (8, scatter), (7, scatter), (3, finish), (6, finish), (5, finish), (8, finish), (7, finish)]
    for t, what in stages:
        what(t)

    pltpu.make_async_copy(pin, pin, t_recv).wait()
    for s in (0, 1):
        block = pin[8 * s : 8 * s + 8].reshape(64, LANES) * keep[s]
        panel_ref[pl.ds(s, 64, stride=2), :] = -block
        hi, lo = split(block)
        p_hi[64 * s : 64 * s + 64, s * LANES : s * LANES + LANES] = hi
        p_lo[64 * s : 64 * s + 64, s * LANES : s * LANES + LANES] = lo

    contract = (((1,), (1,)), ((), ()))
    many = CHIPS // PARTS
    order = OTHERS + [0]

    def c_swap(n):
        span = pl.ds(many * n, many)
        return pltpu.make_async_remote_copy(
            part.at[span, 1 - core], c_take.at[span], cx_send.at[n], cx_recv.at[n], device_id=mate, device_id_type=MESH
        )

    def block(half, i):
        to = in_plane(i) if i else chip
        return half[lax.rem(col - to + 7 + 2 * DEPTH, DEPTH)]

    def c_piece(k):
        i = order[k]
        return pltpu.make_async_remote_copy(
            c_red.at[k], c_got.at[k], c_sems.at[0], c_sems.at[1],
            device_id=(in_plane(i) * 2 + core, col), device_id_type=MESH,
        )

    for n in range(PARTS):
        span = slice(many * n, many * n + many)
        hi = jnp.concatenate([block(lhs_hi, i) for i in order[span]], axis=0)
        lo = jnp.concatenate([block(lhs_lo, i) for i in order[span]], axis=0)
        y = lax.dot_general(hi, p_hi[...], contract, preferred_element_type=jnp.float32)
        y += lax.dot_general(hi, p_lo[...], contract, preferred_element_type=jnp.float32)
        y += lax.dot_general(lo, p_hi[...], contract, preferred_element_type=jnp.float32)
        part[span] = y.reshape(many, 2, 32, LANES)
        c_swap(n).start()
    for n in range(PARTS):
        span = slice(many * n, many * n + many)
        c_swap(n).wait_recv()
        c_red[span] = part[span, core] + c_take[span]
        for k in range(many * n, many * n + many):
            if order[k]:
                c_piece(k).start()
    most = c_got.at[pl.ds(0, CHIPS - 1)]
    pltpu.make_async_copy(most, most, c_sems.at[1]).wait()
    total = c_red[CHIPS - 1]
    for k in range(CHIPS - 1):
        total += c_got[k]
    for s in (0, 1):
        rows = pl.ds(s, 32, stride=2)
        out_ref[rows, :] = diag_ref[rows, :] + total[:, 64 * s : 64 * s + 64]

    for d in hops:
        hops[d].wait_send()
    for t in range(9):
        swap(t).wait_send()
        n = len(signs(t))
        left = got.at[t, pl.ds(1, CHIPS - 1), pl.ds(0, n)]
        pltpu.make_async_copy(left, left, r_send.at[t]).wait()

    @pl.when(chip != col)
    def _():
        pltpu.make_async_copy(pin, pin, t_send).wait()

    @pl.when(chip == col)
    def _():
        left = pin.at[pl.ds(0, CHIPS - 1)]
        pltpu.make_async_copy(left, left, t_send).wait()

    for n in range(PARTS):
        c_swap(n).wait_send()
    pltpu.make_async_copy(most, most, c_sems.at[0]).wait()


def hand_out(panel_in, out_in, panel, out, sems):
    copies = [pltpu.make_async_copy(panel_in, panel, sems.at[0]), pltpu.make_async_copy(out_in, out, sems.at[1])]
    for copy in copies:
        copy.start()
    for copy in copies:
        copy.wait()


def local(ainv_block, factor, block_mask, diag_inverse):
    f = jnp.transpose(factor, (0, 2, 1)).reshape(128, 128)
    diag = diag_inverse.reshape(64, 64)
    f32, bf16 = jnp.float32, jnp.bfloat16
    vmem = pl.BlockSpec(memory_space=pltpu.VMEM)
    dma = pltpu.SemaphoreType.DMA
    panel, out = pl.pallas_call(
        kernel,
        out_shape=(jax.ShapeDtypeStruct((128, 128), f32), jax.ShapeDtypeStruct((64, 64), f32)),
        in_specs=[pl.BlockSpec(memory_space=pltpu.HBM)] * 4,
        out_specs=(vmem, vmem),
        scratch_shapes=[
            pltpu.VMEM((128, 256), f32),
            pltpu.VMEM((128, LANES), f32),
            pltpu.SMEM((2, 32), jnp.int32),
            pltpu.VMEM((64, 64), f32),
            pltpu.VMEM((DEPTH, 128, LANES), f32),
            pltpu.VMEM((DEPTH, 64, 256), bf16),
            pltpu.VMEM((DEPTH, 64, 256), bf16),
            pltpu.VMEM((128, 256), bf16),
            pltpu.VMEM((128, 256), bf16),
            pltpu.VMEM((9, 2, 128, LANES), f32),
            pltpu.VMEM((9, 2, 128, LANES), f32),
            pltpu.VMEM((9, 2, 128, LANES), f32),
            pltpu.VMEM((9, CHIPS, 2, 8, LANES), f32),
            pltpu.VMEM((9, CHIPS, 2, 8, LANES), f32),
            pltpu.VMEM((9, 2, 8, LANES), f32),
            pltpu.VMEM((CHIPS, 8, LANES), f32),
            pltpu.VMEM((128, 256), bf16),
            pltpu.VMEM((128, 256), bf16),
            pltpu.VMEM((DEPTH, 2, 32, LANES), f32),
            pltpu.VMEM((DEPTH, 32, LANES), f32),
            pltpu.VMEM((DEPTH, 32, LANES), f32),
            pltpu.VMEM((CHIPS, 32, LANES), f32),
            dma((4,)), dma((DEPTH + 1,)), dma((DEPTH + 1,)), dma((9,)), dma((9,)), dma((9,)), dma((9,)), dma, dma, dma((PARTS,)), dma((PARTS,)), dma((2,)), pltpu.SemaphoreType.REGULAR,
        ],
        compiler_params=pltpu.CompilerParams(collective_id=0, has_side_effects=True, vmem_limit_bytes=63 * 2**20),
        cost_estimate=pl.CostEstimate(flops=3 * 2 * 84 * 2**20, bytes_accessed=2**20, transcendentals=0),
    )(ainv_block, f, block_mask, diag)
    hbm = pl.BlockSpec(memory_space=pltpu.HBM)
    panel, out = pl.pallas_call(
        hand_out,
        out_shape=(jax.ShapeDtypeStruct((128, 128), f32), jax.ShapeDtypeStruct((64, 64), f32)),
        in_specs=[vmem, vmem],
        out_specs=(hbm, hbm),
        scratch_shapes=[dma((2,))],
    )(panel, out)
    return panel.reshape(64, 2, 128), out.reshape(32, 2, 64)


def solution(mesh):
    placed = (P("row", "col"), P(None, "row", "col"), P(), P("row", None, "col"))
    return jax.shard_map(
        local,
        mesh=mesh,
        in_specs=placed,
        out_specs=(P("col", None, "row"), P("row", None, "col")),
        check_vma=False,
    )
```
